256 devices in a mesh: dp: 32 (over z, x), seq: 8 (over y, core).
Axes of the slice: x: 4, y: 4, z: 8, core: 2. Of those that a mesh axis runs over, the one named last changes fastest.
Arguments:
- source_rows: bfloat16 [32, 8, 288, 3, 3072], P('dp', 'seq'), may hold values from -64 to 64
- shard_counts: int32 [32, 8], P('dp', 'seq'), may hold values from 96 to 288, as said below
- segment_ids: int32 [32, 1536], P('dp', 'seq'), may hold values from 0 to 2, never falling along the last dimension, each value on 1 to 768 neighbouring positions
- out_grad: bfloat16 [32, 1536, 3072], P('dp', 'seq'), may hold values from -6 to 6
Outputs:
- attended: bfloat16 [32, 1536, 3072], P('dp', 'seq')
- packed_grads: bfloat16 [32, 1536, 3, 3072], P('dp', 'seq')
The draws below stay inside these ranges and needn't reach their ends.
Inputs may be any that keep to these rules, and one draw needn't show every extreme that they name: `shard_counts`: for every seq index the counts along dp sum to 6144, and the sum of counts before dp index d differs from d * 192 by at most 48.
All inputs are finite; a program needn't handle non-finite values.
Results may differ from the reference program's by a relative error of at most 0.005.
Values may be sent and summed in bfloat16 or wider, within the bound.
No kernel may reach another device: no remote copies, remote signals or barrier semaphores. Data moves between devices by JAX's collectives and lax.ppermute only.
A program may use at most 128 MiB of HBM per device.

```python
import math
import jax
import jax.numpy as jnp
import numpy as np
from jax import lax

HEADS = 24
HD = 128
TOK_DEV = 192
SEGS = 3
EDGE = 48
SRC_CAP = 288
SLAB = 1536
SEG_MOST = 768
N_DP = 32
N_SEQ = 8


def draw_shard_counts(key, part):
    key = jax.random.fold_in(key, 11)
    inner_key, pick_key = jax.random.split(key)
    interior = jax.random.randint(inner_key, (N_DP - 1, N_SEQ), -EDGE, EDGE + 1)
    chosen = jax.random.randint(pick_key, (1, N_SEQ), 1, N_DP - 2)
    levels = jnp.arange(1, N_DP, dtype=jnp.int32)[:, None]
    interior = jnp.where(levels == chosen, -EDGE, interior)
    interior = jnp.where(levels == chosen + 1, EDGE, interior)
    interior = jnp.where(levels == chosen + 2, -EDGE, interior)
    zeros_row = jnp.zeros((1, N_SEQ), jnp.int32)
    bounds = jnp.concatenate([zeros_row, interior.astype(jnp.int32), zeros_row], axis=0)
    return (TOK_DEV + bounds[1:] - bounds[:-1]).astype(jnp.int32)


def draw_source_rows(key, part):
    key = jax.random.fold_in(key, 23)
    full_shape = (N_DP, N_SEQ, SRC_CAP, 3, HEADS * HD)
    return jnp.clip(jax.random.normal(key, full_shape, jnp.float32), -6.0, 6.0).astype(jnp.bfloat16)


def block_levels(key, dims, cuts, least, top_value):
    factor_of, own = 1.0, jax.random.fold_in(key, 6)
    for axis_at, shards_of in cuts:
        steps = jnp.exp(jax.random.uniform(jax.random.fold_in(own, axis_at), (shards_of,), jnp.float32, least / len(cuts), top_value / len(cuts)))
        factor_of = factor_of * jnp.repeat(steps, dims[axis_at] // shards_of).reshape([-1 if axis == axis_at else 1 for axis in range(len(dims))])
    return factor_of


def split_up(amount, total, bound, skew):
    loads = [(1 << 20) // math.isqrt(rank ** skew) + 1 for rank in range(2, amount + 1)]
    rest, holding = total - bound - (amount - 1), [1] * (amount - 1)
    while rest > 0:
        free = [i for i in range(amount - 1) if holding[i] < bound]
        mass, left = sum([loads[i] for i in free]), rest
        for i in free:
            extra = min(bound - holding[i], max(1, left * loads[i] // mass), rest)
            holding[i] = holding[i] + extra
            rest = rest - extra
    return np.array([bound] + holding)


def ragged(rng, count, total, limit, skew):
    if count == 2:
        one = jax.random.randint(rng, (), max(1, total - limit), min(limit, total - 1) + 1)
        return jnp.stack([one, total - one])
    lengths = jnp.asarray(split_up(count, total, limit, skew), jnp.int32)
    pairs = (count - 1) // 2
    giver, sink = lengths[1:1 + 2 * pairs:2], lengths[2:2 + 2 * pairs:2]
    room = jnp.minimum(giver - 1, limit - sink)
    moved = jax.random.randint(jax.random.fold_in(rng, 1), (pairs,), 0, 1 << 20) % (room + 1)
    lengths = lengths.at[1:1 + 2 * pairs:2].set(giver - moved).at[2:2 + 2 * pairs:2].set(sink + moved)
    return lengths[jax.random.permutation(jax.random.fold_in(rng, 2), count)]


def scatter_about(own_key, extent, deviation, limit, cuts=(), kind=jnp.bfloat16):
    factor_of = block_levels(own_key, extent, cuts, -0.22, 0.18) if cuts else 1.0
    entries = jax.random.normal(own_key, extent, jnp.float32) * deviation * factor_of
    return jnp.minimum(jnp.maximum(entries, -limit), limit).astype(kind)


def setup_inputs(seed: int = 0) -> dict:
    key_of = jax.random.split(jax.random.key(seed), 5)
    return {
        "source_rows": draw_source_rows(jax.random.fold_in(key_of[4], 71), 0),
        "shard_counts": draw_shard_counts(jax.random.fold_in(key_of[4], 71), 0),
        "segment_ids": jax.vmap(lambda own: jnp.searchsorted(jnp.cumsum(ragged(own, SEGS, SLAB, SEG_MOST, 2)), jnp.arange(SLAB), side="right"))(jax.random.split(key_of[2], N_DP)).reshape((N_DP, SLAB)).astype(jnp.int32),
        "out_grad": scatter_about(key_of[3], (N_DP, SLAB, HEADS * HD), 1.0, 6.0, ((0, 32), (1, 8))),
    }


def attend_head(queries, key_rows, value_rows, upstream, labels, factor):
    scores = lax.dot_general(queries, key_rows, (((1,), (1,)), ((), ())), preferred_element_type=jnp.float32) * factor
    same_clip = labels[:, None] == labels[None, :]
    scores = jnp.where(same_clip, scores, -1e30)
    row_top = jnp.max(scores, axis=1, keepdims=True)
    weights = jnp.exp(scores - row_top)
    probs_full = weights / jnp.sum(weights, axis=1, keepdims=True)
    probs_low = probs_full.astype(jnp.bfloat16)
    mixed = jnp.dot(probs_low, value_rows, preferred_element_type=jnp.float32).astype(jnp.bfloat16)
    grad_probs = lax.dot_general(upstream, value_rows, (((1,), (1,)), ((), ())), preferred_element_type=jnp.float32)
    row_inner = jnp.sum(probs_full * grad_probs, axis=1, keepdims=True)
    grad_scores = (probs_full * (grad_probs - row_inner) * factor).astype(jnp.bfloat16)
    grad_queries = jnp.dot(grad_scores, key_rows, preferred_element_type=jnp.float32).astype(jnp.bfloat16)
    grad_keys = lax.dot_general(grad_scores, queries, (((0,), (0,)), ((), ())), preferred_element_type=jnp.float32).astype(jnp.bfloat16)
    grad_values = lax.dot_general(probs_low, upstream, (((0,), (0,)), ((), ())), preferred_element_type=jnp.float32).astype(jnp.bfloat16)
    return mixed, grad_queries, grad_keys, grad_values


def reference(source_rows, shard_counts, segment_ids, out_grad):
    row_width = HEADS * HD
    factor = HD ** -0.5
    positions = jnp.arange(N_DP * TOK_DEV, dtype=jnp.int32)
    shard_ids = jnp.arange(N_DP, dtype=jnp.int32)
    slab_list = []
    for column in range(N_SEQ):
        counts_here = shard_counts[:, column]
        end_rows = jnp.cumsum(counts_here).astype(jnp.int32)
        starts = end_rows - counts_here
        source = jnp.sum((end_rows[None, :] <= positions[:, None]).astype(jnp.int32), axis=1).astype(jnp.int32)
        offset = jnp.sum(jnp.where(shard_ids[None, :] == source[:, None], starts[None, :], 0), axis=1).astype(jnp.int32)
        within = (positions - offset).astype(jnp.int32)
        picked = source_rows[source, column, within]
        slab_list.append(picked.reshape(N_DP, TOK_DEV, 3, row_width))
    packed = jnp.stack(slab_list, axis=1).reshape(N_DP, SLAB, 3, row_width)

    def one_slab(inputs):
        packed_slab, upstream_slab, labels = inputs
        heads_major = packed_slab.reshape(SLAB, 3, HEADS, HD).transpose(2, 0, 1, 3)
        upstream_heads = upstream_slab.reshape(SLAB, HEADS, HD).transpose(1, 0, 2)

        def one_head(entry):
            triple, upstream = entry
            return attend_head(triple[:, 0], triple[:, 1], triple[:, 2], upstream, labels, factor)

        results = lax.map(one_head, (heads_major, upstream_heads))
        stacked = jnp.stack(results, axis=2)
        return stacked.transpose(1, 2, 0, 3).reshape(SLAB, 4, row_width)

    outcome = lax.map(one_slab, (packed, out_grad, segment_ids))
    return outcome[:, :, 0], outcome[:, :, 1:]
```

```python
import functools

import jax
import jax.numpy as jnp
from jax import lax
from jax.experimental import pallas as pl
from jax.experimental.pallas import tpu as pltpu
from jax.sharding import PartitionSpec as P

HD = 128
FACTOR = HD ** (-0.5)
LOG2E = 1.4426950408889634
TILE = 16
VMEM_LIMIT = 48 * 1024 * 1024
NT = (((1,), (1,)), ((), ()))
TN = (((0,), (0,)), ((), ()))
NN = (((1,), (0,)), ((), ()))
ANY = pl.BlockSpec(memory_space=pl.ANY)
WHOLE = pl.BlockSpec(memory_space=pltpu.VMEM)
SCALARS = pl.BlockSpec(memory_space=pltpu.SMEM)


def dot(left, right, dims=NN):
    return lax.dot_general(left, right, dims, preferred_element_type=jnp.float32)


def one_hot(wanted, shape, dtype):
    slot = lax.broadcasted_iota(jnp.int32, shape, 1)
    return jnp.where(slot == wanted, 1.0, 0.0).astype(dtype)


def floor_to(value, step):
    return pl.multiple_of(lax.div(value, step) * step, step)


def shifted(array, axis, by):
    devices = lax.axis_size(axis)
    pairs = [(i, i + by) for i in range(devices) if 0 <= i + by < devices]
    return lax.ppermute(array, axis, pairs)


def edges_kernel(chunks, heads, margin, count_ref, buffer_ref, *refs):
    outs, (window, first, sems) = refs[: 2 * len(chunks)], refs[2 * len(chunks) :]
    capacity = buffer_ref.shape[1]
    reach = window.shape[1]
    start = count_ref[0] - margin
    base = floor_to(jnp.minimum(start, capacity - reach), TILE)
    tail = pltpu.make_async_copy(buffer_ref.at[:, pl.ds(base, reach)], window, sems.at[0])
    head = pltpu.make_async_copy(buffer_ref.at[:, pl.ds(0, margin)], first, sems.at[1])
    tail.start()
    head.start()
    position = lax.broadcasted_iota(jnp.int32, (margin, reach), 0)
    pick = one_hot(position + (start - base), (margin, reach), window.dtype)
    tail.wait()
    head.wait()
    groups = buffer_ref.shape[2] // (heads * HD)
    for part in range(3):
        last = dot(pick, window[part]).astype(window.dtype)
        for which, (at, number) in enumerate(chunks):
            prior, later = outs[2 * which], outs[2 * which + 1]
            wide = number * HD
            for group in range(groups):
                source = (group * heads + at) * HD
                target = group * wide
                prior[part, :, target : target + wide] = last[:, source : source + wide]
                later[part, :, target : target + wide] = first[part, :, source : source + wide]


def edges(live_count, buffer, chunks, heads, margin):
    width = buffer.shape[2]
    shapes = []
    for _, number in chunks:
        shape = (3, margin, width // heads * number)
        shapes += [jax.ShapeDtypeStruct(shape, buffer.dtype)] * 2
    outs = pl.pallas_call(
        functools.partial(edges_kernel, chunks, heads, margin),
        out_shape=shapes,
        in_specs=[SCALARS, ANY],
        out_specs=[WHOLE] * len(shapes),
        scratch_shapes=[
            pltpu.VMEM((3, margin + TILE, width), buffer.dtype),
            pltpu.VMEM((3, margin, width), buffer.dtype),
            pltpu.SemaphoreType.DMA((2,)),
        ],
        compiler_params=pltpu.CompilerParams(vmem_limit_bytes=VMEM_LIMIT),
    )(live_count, buffer)
    return [(outs[2 * i], outs[2 * i + 1]) for i in range(len(chunks))]


def early_start(count, rows):
    return jnp.clip(count - rows * 3 // 4, 0, rows // 4)


def early_kernel(heads, count_ref, buffer_ref, grad_ref, label_ref, out_ref, window, sem):
    rows = grad_ref.shape[0]
    half = rows // 2
    groups = out_ref.shape[0]
    reach = window.shape[1]
    start = early_start(count_ref[0], rows)
    base = floor_to(start, TILE)
    copy = pltpu.make_async_copy(buffer_ref.at[:, pl.ds(base, reach)], window, sem)
    copy.start()
    for group in range(groups):
        for head in range(heads):
            column = (group * heads + head) * HD
            out_ref[group, head * rows : (head + 1) * rows] = grad_ref[:, column : column + HD]
        out_ref[group, heads * rows + heads * 3 * half :] = label_ref[...]
    position = lax.broadcasted_iota(jnp.int32, (half, reach), 0)
    pick = one_hot(position + (start - base), (half, reach), window.dtype)
    copy.wait()
    for part in range(3):
        picked = dot(pick, window[part]).astype(out_ref.dtype)
        for group in range(groups):
            for head in range(heads):
                column = (group * heads + head) * HD
                at = heads * rows + (head * 3 + part) * half
                out_ref[group, at : at + half] = picked[:, column : column + HD]


def early_parts(live_count, buffer, grad, label_tile, groups, heads):
    rows, width = grad.shape
    half = rows // 2
    total = heads * rows + heads * 3 * half + TILE
    return pl.pallas_call(
        functools.partial(early_kernel, heads),
        out_shape=jax.ShapeDtypeStruct((groups, total, HD), grad.dtype),
        in_specs=[SCALARS, ANY, WHOLE, WHOLE],
        out_specs=WHOLE,
        scratch_shapes=[
            pltpu.VMEM((3, half + TILE, width), buffer.dtype),
            pltpu.SemaphoreType.DMA,
        ],
        compiler_params=pltpu.CompilerParams(vmem_limit_bytes=VMEM_LIMIT),
    )(live_count, buffer, grad, label_tile)


def rest_kernel(chunk, heads, where_ref, prior_ref, buffer_ref, later_ref, out_ref, joined, sems):
    at, number = chunk
    groups = out_ref.shape[0]
    margin = prior_ref.shape[1]
    rows = 4 * margin
    half = 2 * margin
    wide = number * HD
    lead, count = where_ref[0], where_ref[1]
    own_end = count + lead
    start = early_start(count, rows)
    place = start + lead
    base = floor_to(start + half, TILE)
    reach = half + TILE
    copies = [
        pltpu.make_async_copy(prior_ref, joined.at[:, pl.ds(0, margin)], sems.at[0]),
        pltpu.make_async_copy(later_ref, joined.at[:, pl.ds(half + reach, margin)], sems.at[1]),
    ]
    for group in range(groups):
        columns = pl.ds((group * heads + at) * HD, wide)
        target = pl.ds(group * wide, wide)
        copies.append(
            pltpu.make_async_copy(
                buffer_ref.at[:, pl.ds(0, margin), columns],
                joined.at[:, pl.ds(margin, margin), target],
                sems.at[len(copies)],
            )
        )
        copies.append(
            pltpu.make_async_copy(
                buffer_ref.at[:, pl.ds(base, reach), columns],
                joined.at[:, pl.ds(half, reach), target],
                sems.at[len(copies)],
            )
        )
    for copy in copies:
        copy.start()
    shape = (half, joined.shape[1])
    slot = lax.broadcasted_iota(jnp.int32, shape, 0)
    position = jnp.where(slot < place, slot, slot + half)
    own_row = position - lead
    wanted = jnp.where(
        position >= own_end,
        position - own_end + half + reach,
        jnp.where(slot < place, own_row + margin, own_row - base + half),
    )
    pick = one_hot(wanted, shape, joined.dtype)
    place_tile = jnp.full((TILE, HD), place, jnp.int32).astype(jnp.float32).astype(out_ref.dtype)
    for copy in copies:
        copy.wait()
    for part in range(3):
        picked = dot(pick, joined[part]).astype(out_ref.dtype)
        for group in range(groups):
            for head in range(number):
                column = (group * number + head) * HD
                to = (head * 3 + part) * half
                out_ref[group, to : to + half] = picked[:, column : column + HD]
    for group in range(groups):
        out_ref[group, number * 3 * half :] = place_tile


def rest_parts(chunk, heads, where, prior, buffer, later, groups):
    margin = prior.shape[1]
    wide = prior.shape[2]
    total = chunk[1] * 6 * margin + TILE
    return pl.pallas_call(
        functools.partial(rest_kernel, chunk, heads),
        out_shape=jax.ShapeDtypeStruct((groups, total, HD), buffer.dtype),
        in_specs=[SCALARS, ANY, ANY, ANY],
        out_specs=WHOLE,
        scratch_shapes=[
            pltpu.VMEM((3, 5 * margin + TILE, wide), buffer.dtype),
            pltpu.SemaphoreType.DMA((2 * groups + 2,)),
        ],
        compiler_params=pltpu.CompilerParams(vmem_limit_bytes=VMEM_LIMIT),
    )(where, prior, buffer, later)


def clip_of(position, first_end, second_end):
    return jnp.where(position >= first_end, 1, 0) + jnp.where(position >= second_end, 1, 0)


def attend_kernel(
    early_ref,
    rest_ref,
    place_ref,
    upstream_ref,
    label_ref,
    out_ref,
    query_rows,
    key_rows,
    value_rows,
    grad_keys,
    grad_values,
):
    groups, rows, _ = upstream_ref.shape
    half = rows // 2
    total = groups * rows
    pair = 2
    block = pair * rows
    labels = label_ref[...].astype(jnp.float32)
    first_end = jnp.sum(jnp.where(labels < 0.5, 1.0, 0.0)).astype(jnp.int32)
    second_end = jnp.sum(jnp.where(labels < 1.5, 1.0, 0.0)).astype(jnp.int32)
    grad_keys[...] = jnp.zeros_like(grad_keys)
    grad_values[...] = jnp.zeros_like(grad_values)

    for group in range(groups):
        place = jnp.max(place_ref[group].astype(jnp.float32)).astype(jnp.int32)
        position = lax.broadcasted_iota(jnp.int32, (rows, rows), 0)
        wanted = jnp.where(
            position < place,
            position + half,
            jnp.where(position < place + half, position - place, position),
        )
        pick = one_hot(wanted, (rows, rows), early_ref.dtype)
        parts = [
            jnp.concatenate(
                [
                    early_ref[group, part * half : (part + 1) * half],
                    rest_ref[group, part * half : (part + 1) * half],
                ],
                axis=0,
            )
            for part in range(3)
        ]
        whole = dot(pick, jnp.concatenate(parts, axis=1)).astype(early_ref.dtype)
        span = pl.ds(group * rows, rows)
        query_rows[span] = whole[:, :HD]
        key_rows[span] = whole[:, HD : 2 * HD]
        value_rows[span] = whole[:, 2 * HD :]

    def on_keys(i, low, reach):
        begin = pl.multiple_of(jnp.minimum(low, total - reach), HD) if reach < total else 0
        keys = pl.ds(begin, reach)
        queries = query_rows[pl.ds(pl.multiple_of(i * block, block), block)]
        upstream = upstream_ref[pl.ds(i * pair, pair)].reshape(block, HD)
        scores = dot(queries, key_rows[keys], NT)
        grad_probs = dot(upstream, value_rows[keys], NT)
        row_at = i * block + lax.broadcasted_iota(jnp.int32, (block, 1), 0)
        key_at = begin + lax.broadcasted_iota(jnp.int32, (1, reach), 1)
        same_clip = clip_of(row_at, first_end, second_end) == clip_of(key_at, first_end, second_end)
        scores = jnp.where(same_clip, scores, -1e30)
        row_top = jnp.max(scores, axis=1, keepdims=True)
        weights = jnp.exp2((scores - row_top) * (FACTOR * LOG2E))
        probs = weights * (1.0 / jnp.sum(weights, axis=1, keepdims=True))
        probs_low = probs.astype(jnp.bfloat16)
        row_inner = jnp.sum(probs * grad_probs, axis=1, keepdims=True)
        grad_scores = (probs * (grad_probs - row_inner) * FACTOR).astype(jnp.bfloat16)
        mixed = dot(probs_low, value_rows[keys]).astype(out_ref.dtype)
        grad_queries = dot(grad_scores, key_rows[keys]).astype(out_ref.dtype)
        out_ref[pl.ds(i * pair, pair), 0, 0] = mixed.reshape(pair, rows, HD)
        out_ref[pl.ds(i * pair, pair), 0, 1] = grad_queries.reshape(pair, rows, HD)
        grad_keys[:, keys] += dot(queries, grad_scores, TN)
        grad_values[:, keys] += dot(upstream, probs_low, TN)

    def one(i, carry):
        begin = i * block
        last = begin + block - 1
        low = jnp.where(
            begin >= second_end, second_end, jnp.where(begin >= first_end, first_end, 0)
        )
        high = jnp.where(
            last < first_end, first_end, jnp.where(last < second_end, second_end, total)
        )
        low = lax.div(low, HD) * HD
        span = high - low
        covered = 0
        for reach in (total // 3, total // 2 + HD, total):
            pl.when((span > covered) & (span <= reach))(functools.partial(on_keys, i, low, reach))
            covered = reach
        return carry

    lax.fori_loop(0, groups // pair, one, 0)
    out_ref[:, 0, 2] = grad_keys[...].T.reshape(groups, rows, HD).astype(out_ref.dtype)
    out_ref[:, 0, 3] = grad_values[...].T.reshape(groups, rows, HD).astype(out_ref.dtype)


def attend(chunk, heads, early, rest, rows):
    at, number = chunk
    groups = early.shape[0]
    total = groups * rows
    half = rows // 2
    early_at = heads * rows // (3 * half)
    label_at = heads * (rows + 3 * half) // TILE
    place_at = number * 3 * half // TILE
    return pl.pallas_call(
        attend_kernel,
        out_shape=jax.ShapeDtypeStruct((groups, number, 4, rows, HD), early.dtype),
        grid=(number,),
        in_specs=[
            pl.BlockSpec((groups, 3 * half, HD), lambda h: (0, early_at + at + h, 0)),
            pl.BlockSpec((groups, 3 * half, HD), lambda h: (0, h, 0)),
            pl.BlockSpec((groups, TILE, HD), lambda h: (0, place_at, 0)),
            pl.BlockSpec((groups, rows, HD), lambda h: (0, at + h, 0)),
            pl.BlockSpec((groups, TILE, HD), lambda h: (0, label_at, 0)),
        ],
        out_specs=pl.BlockSpec((groups, 1, 4, rows, HD), lambda h: (0, h, 0, 0, 0)),
        scratch_shapes=[pltpu.VMEM((total, HD), early.dtype)] * 3
        + [pltpu.VMEM((HD, total), jnp.float32)] * 2,
        compiler_params=pltpu.CompilerParams(vmem_limit_bytes=VMEM_LIMIT),
        cost_estimate=pl.CostEstimate(
            flops=10 * number * total * total * HD,
            bytes_accessed=16 * number * total * HD,
            transcendentals=number * total * total,
        ),
    )(early, rest, rest, early, early)


def unpack_kernel(chunk, heads, part_ref, *refs):
    attended_ref, grads_ref, sems = refs[-3:]
    at, number = chunk
    copies = []
    for group in range(part_ref.shape[0]):
        for head in range(number):
            columns = pl.ds((group * heads + at + head) * HD, HD)
            one = part_ref.at[group, head, 0]
            three = part_ref.at[group, head, pl.ds(1, 3)]
            where = len(copies)
            copies.append(
                pltpu.make_async_copy(one, attended_ref.at[:, columns], sems.at[where])
            )
            copies.append(
                pltpu.make_async_copy(three, grads_ref.at[:, :, columns], sems.at[where + 1])
            )
    for copy in copies:
        copy.start()
    for copy in copies:
        copy.wait()


def unpack(chunk, heads, part, so_far):
    groups, number, _, rows, _ = part.shape
    width = groups * heads * HD
    return pl.pallas_call(
        functools.partial(unpack_kernel, chunk, heads),
        out_shape=[
            jax.ShapeDtypeStruct((rows, width), part.dtype),
            jax.ShapeDtypeStruct((3, rows, width), part.dtype),
        ],
        in_specs=[WHOLE] + [ANY] * len(so_far),
        out_specs=[ANY, ANY],
        scratch_shapes=[pltpu.SemaphoreType.DMA((2 * groups * number,))],
        input_output_aliases={1: 0, 2: 1} if so_far else {},
        compiler_params=pltpu.CompilerParams(vmem_limit_bytes=VMEM_LIMIT),
    )(part, *so_far)


def exchange(array):
    return lax.all_to_all(array, "seq", split_axis=0, concat_axis=0, tiled=True)


def local(source_rows, shard_counts, segment_ids, out_grad):
    buffer = source_rows[0, 0].transpose(1, 0, 2)
    live_count = shard_counts[0]
    slab_rows = out_grad.shape[1]
    margin = slab_rows // 4
    groups = lax.axis_size("seq")
    heads = out_grad.shape[2] // HD // groups
    chunks = [(0, 1), (1, heads - 1)]
    shard_index = lax.axis_index("dp")

    label_tile = jnp.pad(
        segment_ids[0].astype(jnp.bfloat16),
        (0, TILE * HD - slab_rows),
        constant_values=3,
    ).reshape(TILE, HD)
    message = early_parts(live_count, buffer, out_grad[0], label_tile, groups, heads)
    early = exchange(message)
    message, live_count = lax.optimization_barrier((message, live_count))
    ends = edges(live_count, buffer, chunks, heads, margin)
    halos = [(shifted(ends[0][0], "dp", 1), shifted(ends[0][1], "dp", -1))]

    first_ends, own_count = lax.optimization_barrier((ends[0], live_count))
    counts = lax.all_gather(own_count, "dp", tiled=True)
    below = jnp.arange(counts.shape[0], dtype=jnp.int32) < shard_index
    lead_rows = jnp.sum(jnp.where(below, counts, 0)) - shard_index * slab_rows
    where = jnp.stack([lead_rows, live_count[0]]).astype(jnp.int32)

    later_ends, where = lax.optimization_barrier((ends[1:], where))
    for prior, later in later_ends:
        halos.append((shifted(prior, "dp", 1), shifted(later, "dp", -1)))

    received = []
    for chunk, (prior, later) in zip(chunks, halos):
        rest = rest_parts(chunk, heads, where, prior, buffer, later, groups)
        rest, early = lax.optimization_barrier((rest, early))
        received.append(exchange(rest))
    result = ()
    for chunk, rest in zip(chunks, received):
        returned = exchange(attend(chunk, heads, early, rest, slab_rows))
        result = unpack(chunk, heads, returned, result)
    attended, grads = result
    return attended[None], grads.transpose(1, 0, 2)[None]


def solution(mesh):
    placed = (
        P("dp", "seq", None, None, None),
        P("dp", "seq"),
        P("dp", "seq"),
        P("dp", "seq", None),
    )
    return jax.shard_map(
        local,
        mesh=mesh,
        in_specs=placed,
        out_specs=(P("dp", "seq", None), P("dp", "seq", None, None)),
        check_vma=False,
    )
```

```python
import functools

import jax
import jax.numpy as jnp
from jax import lax
from jax.experimental import pallas as pl
from jax.experimental.pallas import tpu as pltpu
from jax.sharding import PartitionSpec as P

HD = 128
FACTOR = HD ** (-0.5)
LOG2E = 1.4426950408889634
TILE = 16
VMEM_LIMIT = 64 * 1024 * 1024 - 256 * 1024
NT = (((1,), (1,)), ((), ()))
TN = (((0,), (0,)), ((), ()))
NN = (((1,), (0,)), ((), ()))
HBM = pl.BlockSpec(memory_space=pltpu.HBM)
ANY = pl.BlockSpec(memory_space=pl.ANY)
WHOLE = pl.BlockSpec(memory_space=pltpu.VMEM)
SCALARS = pl.BlockSpec(memory_space=pltpu.SMEM)


def dot(left, right, dims=NN):
    return lax.dot_general(left, right, dims, preferred_element_type=jnp.float32)


def one_hot(wanted, shape, dtype):
    slot = lax.broadcasted_iota(jnp.int32, shape, 1)
    return jnp.where(slot == wanted, 1.0, 0.0).astype(dtype)


def floor_to(value, step):
    return pl.multiple_of(lax.div(value, step) * step, step)


def shifted(array, axis, by):
    devices = lax.axis_size(axis)
    pairs = [(i, i + by) for i in range(devices) if 0 <= i + by < devices]
    return lax.ppermute(array, axis, pairs)


def early_start(count, rows):
    return jnp.clip(count - rows * 3 // 4, 0, rows // 4)


def first_kernel(chunks, heads, count_ref, buffer_ref, grad_ref, label_ref, out_ref, *refs):
    ends, refs = refs[: 2 * len(chunks)], refs[2 * len(chunks) :]
    message, window, grad, tail, head, labels, sems = refs[:7]
    priors = refs[7:]
    rows = grad.shape[0]
    half = rows // 2
    margin = head.shape[1]
    capacity = buffer_ref.shape[1]
    groups = out_ref.shape[0]
    count = count_ref[0]
    start = early_start(count, rows)
    base = floor_to(start, TILE)
    reach = window.shape[1]
    tail_start = count - margin
    tail_reach = tail.shape[1]
    tail_base = floor_to(jnp.minimum(tail_start, capacity - tail_reach), TILE)
    copies = [
        pltpu.make_async_copy(grad_ref, grad, sems.at[0]),
        pltpu.make_async_copy(buffer_ref.at[:, pl.ds(base, reach)], window, sems.at[1]),
        pltpu.make_async_copy(buffer_ref.at[:, pl.ds(tail_base, tail_reach)], tail, sems.at[2]),
        pltpu.make_async_copy(buffer_ref.at[:, pl.ds(0, margin)], head, sems.at[3]),
    ]
    for copy in copies:
        copy.start()
    labels[...] = jnp.full(labels.shape, 3.0, jnp.float32)
    for at in range(0, rows, HD):
        wide = min(HD, rows - at)
        labels[at // HD : at // HD + 1, :wide] = label_ref[:, at : at + wide].astype(jnp.float32)
    label_tile = labels[...].astype(out_ref.dtype)
    position = lax.broadcasted_iota(jnp.int32, (half, reach), 0)
    pick = one_hot(position + (start - base), (half, reach), window.dtype)
    sent = []
    copies[0].wait()
    copies[1].wait()
    for group in range(groups):
        columns = slice(group * heads * HD, (group + 1) * heads * HD)
        for h in range(heads):
            column = (group * heads + h) * HD
            message[group, h * rows : (h + 1) * rows] = grad[:, column : column + HD]
        for part in range(3):
            picked = dot(pick, window[part, :, columns]).astype(out_ref.dtype)
            for h in range(heads):
                at = heads * rows + (h * 3 + part) * half
                message[group, at : at + half] = picked[:, h * HD : (h + 1) * HD]
        message[group, heads * (rows + 3 * half) :] = label_tile
        sent.append(pltpu.make_async_copy(message.at[group], out_ref.at[group], sems.at[4 + group]))
        sent[-1].start()
    copies[2].wait()
    copies[3].wait()
    free = 4 + groups
    position = lax.broadcasted_iota(jnp.int32, (margin, tail_reach), 0)
    pick = one_hot(position + (tail_start - tail_base), (margin, tail_reach), tail.dtype)
    for which, (at, number) in enumerate(chunks):
        wide = number * HD
        for group in range(groups):
            source = (group * heads + at) * HD
            target = group * wide
            sent.append(
                pltpu.make_async_copy(
                    head.at[:, :, pl.ds(source, wide)],
                    ends[2 * which + 1].at[:, :, pl.ds(target, wide)],
                    sems.at[free],
                )
            )
            sent[-1].start()
            free += 1
            for part in range(3):
                last = dot(pick, tail[part, :, source : source + wide])
                priors[which][part, :, target : target + wide] = last.astype(tail.dtype)
        sent.append(pltpu.make_async_copy(priors[which], ends[2 * which], sems.at[free]))
        sent[-1].start()
        free += 1
    for copy in sent:
        copy.wait()


def first_parts(live_count, buffer, grad, labels, chunks, groups, heads, margin):
    rows, width = grad.shape
    half = rows // 2
    shapes = [(groups, heads * rows + heads * 3 * half + TILE, HD)]
    priors = []
    for _, number in chunks:
        shape = (3, margin, width // heads * number)
        shapes += [shape, shape]
        priors.append(pltpu.VMEM(shape, buffer.dtype))
    outs = pl.pallas_call(
        functools.partial(first_kernel, chunks, heads),
        out_shape=[jax.ShapeDtypeStruct(shape, buffer.dtype) for shape in shapes],
        in_specs=[SCALARS, HBM, HBM, WHOLE],
        out_specs=[HBM] * len(shapes),
        scratch_shapes=[
            pltpu.VMEM(shapes[0], buffer.dtype),
            pltpu.VMEM((3, half + TILE, width), buffer.dtype),
            pltpu.VMEM((rows, width), grad.dtype),
            pltpu.VMEM((3, margin + TILE, width), buffer.dtype),
            pltpu.VMEM((3, margin, width), buffer.dtype),
            pltpu.VMEM((TILE, HD), jnp.float32),
            pltpu.SemaphoreType.DMA((4 + groups + len(chunks) * (groups + 1),)),
        ]
        + priors,
        compiler_params=pltpu.CompilerParams(vmem_limit_bytes=VMEM_LIMIT),
    )(live_count, buffer, grad, labels)
    return outs[0], [(outs[1 + 2 * i], outs[2 + 2 * i]) for i in range(len(chunks))]


def rest_kernel(chunk, heads, counts_ref, shard_ref, prior_ref, buffer_ref, later_ref, out_ref, message, joined, sems):
    at, number = chunk
    groups = out_ref.shape[0]
    margin = prior_ref.shape[1]
    rows = 4 * margin
    half = 2 * margin
    wide = number * HD
    shard = shard_ref[0]
    count = counts_ref[shard]
    before = lax.fori_loop(0, shard, lambda i, total: total + counts_ref[i], jnp.int32(0))
    lead = before - shard * rows
    own_end = count + lead
    start = early_start(count, rows)
    place = start + lead
    base = floor_to(start + half, TILE)
    reach = half + TILE
    copies = [
        pltpu.make_async_copy(prior_ref, joined.at[:, pl.ds(0, margin)], sems.at[0]),
        pltpu.make_async_copy(later_ref, joined.at[:, pl.ds(half + reach, margin)], sems.at[1]),
    ]
    for group in range(groups):
        columns = pl.ds((group * heads + at) * HD, wide)
        target = pl.ds(group * wide, wide)
        copies.append(
            pltpu.make_async_copy(
                buffer_ref.at[:, pl.ds(0, margin), columns],
                joined.at[:, pl.ds(margin, margin), target],
                sems.at[len(copies)],
            )
        )
        copies.append(
            pltpu.make_async_copy(
                buffer_ref.at[:, pl.ds(base, reach), columns],
                joined.at[:, pl.ds(half, reach), target],
                sems.at[len(copies)],
            )
        )
    for copy in copies:
        copy.start()
    shape = (half, joined.shape[1])
    slot = lax.broadcasted_iota(jnp.int32, shape, 0)
    position = jnp.where(slot < place, slot, slot + half)
    own_row = position - lead
    wanted = jnp.where(
        position >= own_end,
        position - own_end + half + reach,
        jnp.where(slot < place, own_row + margin, own_row - base + half),
    )
    pick = one_hot(wanted, shape, joined.dtype)
    place_tile = jnp.full((TILE, HD), place, jnp.int32).astype(jnp.float32).astype(out_ref.dtype)
    sent = []
    for copy in copies:
        copy.wait()
    for group in range(groups):
        for part in range(3):
            source = joined[part, :, group * wide : (group + 1) * wide]
            picked = dot(pick, source).astype(out_ref.dtype)
            for head in range(number):
                to = (head * 3 + part) * half
                message[group, to : to + half] = picked[:, head * HD : (head + 1) * HD]
        message[group, number * 3 * half :] = place_tile
        sent.append(
            pltpu.make_async_copy(
                message.at[group], out_ref.at[group], sems.at[2 * groups + 2 + group]
            )
        )
        sent[-1].start()
    for copy in sent:
        copy.wait()


def rest_parts(chunk, heads, counts, shard, prior, buffer, later, groups):
    margin = prior.shape[1]
    wide = prior.shape[2]
    total = chunk[1] * 6 * margin + TILE
    return pl.pallas_call(
        functools.partial(rest_kernel, chunk, heads),
        out_shape=jax.ShapeDtypeStruct((groups, total, HD), buffer.dtype),
        in_specs=[SCALARS, SCALARS, ANY, HBM, ANY],
        out_specs=HBM,
        scratch_shapes=[
            pltpu.VMEM((groups, total, HD), buffer.dtype),
            pltpu.VMEM((3, 5 * margin + TILE, wide), buffer.dtype),
            pltpu.SemaphoreType.DMA((3 * groups + 2,)),
        ],
        compiler_params=pltpu.CompilerParams(vmem_limit_bytes=VMEM_LIMIT),
    )(counts, shard, prior, buffer, later)


def clip_of(position, first_end, second_end):
    return jnp.where(position >= first_end, 1, 0) + jnp.where(position >= second_end, 1, 0)


def attend_kernel(
    early_ref,
    rest_ref,
    place_ref,
    upstream_ref,
    label_ref,
    place_in_seq_ref,
    *refs,
):
    outs, refs = refs[:-7], refs[-7:]
    query_rows, key_rows, value_rows, grad_keys, grad_values, results, sems = refs
    groups, rows, _ = upstream_ref.shape
    half = rows // 2
    total = groups * rows
    pair = 2
    block = pair * rows
    labels = label_ref[...].astype(jnp.float32)
    first_end = jnp.sum(jnp.where(labels < 0.5, 1.0, 0.0)).astype(jnp.int32)
    second_end = jnp.sum(jnp.where(labels < 1.5, 1.0, 0.0)).astype(jnp.int32)
    grad_keys[...] = jnp.zeros_like(grad_keys)
    grad_values[...] = jnp.zeros_like(grad_values)

    for group in range(groups):
        place = jnp.max(place_ref[group].astype(jnp.float32)).astype(jnp.int32)
        position = lax.broadcasted_iota(jnp.int32, (rows, rows), 0)
        wanted = jnp.where(
            position < place,
            position + half,
            jnp.where(position < place + half, position - place, position),
        )
        pick = one_hot(wanted, (rows, rows), early_ref.dtype)
        parts = [
            jnp.concatenate(
                [
                    early_ref[group, part * half : (part + 1) * half],
                    rest_ref[group, part * half : (part + 1) * half],
                ],
                axis=0,
            )
            for part in range(3)
        ]
        whole = dot(pick, jnp.concatenate(parts, axis=1)).astype(early_ref.dtype)
        span = pl.ds(group * rows, rows)
        query_rows[span] = whole[:, :HD]
        key_rows[span] = whole[:, HD : 2 * HD]
        value_rows[span] = whole[:, 2 * HD :]

    def on_keys(i, low, reach):
        begin = pl.multiple_of(jnp.minimum(low, total - reach), HD) if reach < total else 0
        keys = pl.ds(begin, reach)
        queries = query_rows[pl.ds(pl.multiple_of(i * block, block), block)]
        upstream = upstream_ref[pl.ds(i * pair, pair)].reshape(block, HD)
        scores = dot(queries, key_rows[keys], NT)
        grad_probs = dot(upstream, value_rows[keys], NT)
        row_at = i * block + lax.broadcasted_iota(jnp.int32, (block, 1), 0)
        key_at = begin + lax.broadcasted_iota(jnp.int32, (1, reach), 1)
        same_clip = clip_of(row_at, first_end, second_end) == clip_of(key_at, first_end, second_end)
        scores = jnp.where(same_clip, scores, -1e30)
        row_top = jnp.max(scores, axis=1, keepdims=True)
        weights = jnp.exp2((scores - row_top) * (FACTOR * LOG2E))
        probs = weights * (1.0 / jnp.sum(weights, axis=1, keepdims=True))
        probs_low = probs.astype(jnp.bfloat16)
        row_inner = jnp.sum(probs * grad_probs, axis=1, keepdims=True)
        grad_scores = (probs * (grad_probs - row_inner) * FACTOR).astype(jnp.bfloat16)
        mixed = dot(probs_low, value_rows[keys]).astype(results.dtype)
        grad_queries = dot(grad_scores, key_rows[keys]).astype(results.dtype)
        results[pl.ds(i * pair, pair), 0] = mixed.reshape(pair, rows, HD)
        results[pl.ds(i * pair, pair), 1] = grad_queries.reshape(pair, rows, HD)
        grad_keys[:, keys] += dot(queries, grad_scores, TN)
        grad_values[:, keys] += dot(upstream, probs_low, TN)

    def one(i, carry):
        begin = i * block
        last = begin + block - 1
        low = jnp.where(
            begin >= second_end, second_end, jnp.where(begin >= first_end, first_end, 0)
        )
        high = jnp.where(
            last < first_end, first_end, jnp.where(last < second_end, second_end, total)
        )
        low = lax.div(low, HD) * HD
        span = high - low
        covered = 0
        for reach in (total // 3, total // 2 + HD, total):
            pl.when((span > covered) & (span <= reach))(functools.partial(on_keys, i, low, reach))
            covered = reach
        return carry

    lax.fori_loop(0, groups // pair, one, 0)
    results[:, 2] = grad_keys[...].T.reshape(groups, rows, HD).astype(results.dtype)
    results[:, 3] = grad_values[...].T.reshape(groups, rows, HD).astype(results.dtype)
    copies = []
    if len(outs) == 1:
        copies.append(pltpu.make_async_copy(results, outs[0], sems.at[0]))
    for ahead, out in enumerate(outs if len(outs) > 1 else ()):
        for other in range(2):
            source = results.at[group_at(place_in_seq_ref[0], groups, ahead, other)]
            sem = sems.at[len(copies)]
            copies.append(pltpu.make_async_copy(source, out.at[other], sem))
    for copy in copies:
        copy.start()
    for copy in copies:
        copy.wait()


def group_at(place, groups, ahead, other):
    core = lax.rem(place, 2)
    chip = lax.rem(lax.div(place, 2) + ahead, groups // 2)
    return 2 * chip + (1 - core if other else core)


def attend(head, local_head, heads, early, rest, rows, place, parted):
    groups = early.shape[0]
    total = groups * rows
    half = rows // 2
    early_at = heads * rows // (3 * half)
    label_at = heads * (rows + 3 * half) // TILE
    place_at = rest.shape[1] // TILE - 1
    if parted:
        shapes = [(2, 4, rows, HD)] * (groups // 2)
    else:
        shapes = [(groups, 4, rows, HD)]
    return pl.pallas_call(
        attend_kernel,
        out_shape=[jax.ShapeDtypeStruct(shape, early.dtype) for shape in shapes],
        grid=(1,),
        in_specs=[
            pl.BlockSpec((groups, 3 * half, HD), lambda h: (0, early_at + head, 0)),
            pl.BlockSpec((groups, 3 * half, HD), lambda h: (0, local_head, 0)),
            pl.BlockSpec((groups, TILE, HD), lambda h: (0, place_at, 0)),
            pl.BlockSpec((groups, rows, HD), lambda h: (0, head, 0)),
            pl.BlockSpec((groups, TILE, HD), lambda h: (0, label_at, 0)),
            SCALARS,
        ],
        out_specs=[HBM] * len(shapes),
        scratch_shapes=[pltpu.VMEM((total, HD), early.dtype)] * 3
        + [pltpu.VMEM((HD, total), jnp.float32)] * 2
        + [pltpu.VMEM((groups, 4, rows, HD), early.dtype), pltpu.SemaphoreType.DMA((groups,))],
        compiler_params=pltpu.CompilerParams(vmem_limit_bytes=VMEM_LIMIT),
        cost_estimate=pl.CostEstimate(
            flops=10 * total * total * HD,
            bytes_accessed=16 * total * HD,
            transcendentals=total * total,
        ),
    )(early, rest, rest, early, early, place)


def others_kernel(*refs):
    parts, out_ref, held, sems = refs[:-3], refs[-3], refs[-2], refs[-1]
    number = len(parts)
    loads = []
    for i, part in enumerate(parts):
        loads.append(pltpu.make_async_copy(part.at[1], held.at[i], sems.at[i]))
        loads[-1].start()
    stores = []
    for i in range(number):
        loads[i].wait()
        stores.append(pltpu.make_async_copy(held.at[i], out_ref.at[i], sems.at[number + i]))
        stores[-1].start()
    for store in stores:
        store.wait()


def others_of(parts):
    shape = (len(parts), *parts[0].shape[1:])
    return pl.pallas_call(
        others_kernel,
        out_shape=jax.ShapeDtypeStruct(shape, parts[0].dtype),
        in_specs=[ANY] * len(parts),
        out_specs=HBM,
        scratch_shapes=[
            pltpu.VMEM(shape, parts[0].dtype),
            pltpu.SemaphoreType.DMA((2 * len(parts),)),
        ],
        compiler_params=pltpu.CompilerParams(vmem_limit_bytes=VMEM_LIMIT),
    )(*parts)


def unpack_kernel(head, heads, groups, other, number, place_ref, *refs):
    sources = refs[:number]
    attended_ref, grads_ref, held, sems = refs[-4:]
    blocks = []
    if other is None:
        blocks = [(sources[0].at[group], group) for group in range(groups)]
    for back in range(0 if other is None else groups // 2):
        ahead = (groups // 2 - back) % (groups // 2)
        block = sources[0].at[back] if other else sources[back].at[0]
        blocks.append((block, group_at(place_ref[0], groups, ahead, other)))
    loads = []
    for i, (block, _) in enumerate(blocks):
        loads.append(pltpu.make_async_copy(block, held.at[i], sems.at[i]))
        loads[-1].start()
    stores = []
    for i, (_, group) in enumerate(blocks):
        loads[i].wait()
        columns = pl.ds(pl.multiple_of((group * heads + head) * HD, HD), HD)
        first = sems.at[len(blocks) + 2 * i]
        second = sems.at[len(blocks) + 2 * i + 1]
        stores.append(pltpu.make_async_copy(held.at[i, 0], attended_ref.at[:, columns], first))
        stores.append(
            pltpu.make_async_copy(held.at[i, pl.ds(1, 3)], grads_ref.at[:, :, columns], second)
        )
        stores[-2].start()
        stores[-1].start()
    for store in stores:
        store.wait()


def unpack(head, heads, groups, place, sources, other, so_far):
    _, _, rows, _ = sources[0].shape
    width = groups * heads * HD
    dtype = sources[0].dtype
    number = len(sources)
    return pl.pallas_call(
        functools.partial(unpack_kernel, head, heads, groups, other, number),
        out_shape=[
            jax.ShapeDtypeStruct((rows, width), dtype),
            jax.ShapeDtypeStruct((3, rows, width), dtype),
        ],
        in_specs=[SCALARS] + [ANY] * number + [HBM] * len(so_far),
        out_specs=[HBM, HBM],
        scratch_shapes=[
            pltpu.VMEM((groups, 4, rows, HD), dtype),
            pltpu.SemaphoreType.DMA((3 * groups,)),
        ],
        input_output_aliases={1 + number: 0, 2 + number: 1} if so_far else {},
        compiler_params=pltpu.CompilerParams(vmem_limit_bytes=VMEM_LIMIT),
    )(place, *sources, *so_far)


def to_chips(parts):
    places = lax.axis_size("seq")
    arrived = [parts[0]]
    for ahead in range(1, len(parts)):
        pairs = [(i, (i + 2 * ahead) % places) for i in range(places)]
        arrived.append(lax.ppermute(parts[ahead], "seq", pairs))
    return arrived


def to_cores(arrived):
    swap = [(i, i ^ 1) for i in range(lax.axis_size("seq"))]
    return lax.ppermute(others_of(arrived), "seq", swap)


def after(array, first):
    return lax.optimization_barrier((array, first))[0]


def exchange(array):
    return lax.all_to_all(array, "seq", split_axis=0, concat_axis=0, tiled=True)


def local(source_rows, shard_counts, segment_ids, out_grad):
    buffer = source_rows[0, 0].transpose(1, 0, 2)
    live_count = shard_counts[0]
    slab_rows = out_grad.shape[1]
    margin = slab_rows // 4
    groups = lax.axis_size("seq")
    heads = out_grad.shape[2] // HD // groups
    chunks = [(0, 1), (1, heads - 1)]
    shard = lax.axis_index("dp").astype(jnp.int32)[None]
    place = lax.axis_index("seq").astype(jnp.int32)[None]

    message, ends = first_parts(
        live_count, buffer, out_grad[0], segment_ids, chunks, groups, heads, margin
    )
    early = exchange(message)
    first_ends, own_count = lax.optimization_barrier((ends[0], live_count))
    halos = [(shifted(first_ends[0], "dp", 1), shifted(first_ends[1], "dp", -1))]
    indices = jnp.arange(lax.axis_size("dp"), dtype=jnp.int32)
    counts = lax.psum(jnp.where(indices == shard, own_count, 0), "dp")
    later_ends, counts = lax.optimization_barrier((ends[1:], counts))
    for prior, later in later_ends:
        halos.append((shifted(prior, "dp", 1), shifted(later, "dp", -1)))

    received = []
    for chunk, (prior, later) in zip(chunks, halos):
        rest = rest_parts(chunk, heads, counts, shard, prior, buffer, later, groups)
        rest, early = lax.optimization_barrier((rest, early))
        received.append(exchange(rest))
    rest_a, rest_b = received
    blocks_a = attend(0, 0, heads, early, rest_a, slab_rows, place, True)
    arrived_a = to_chips(blocks_a)
    rest_b = after(rest_b, blocks_a)
    blocks_b = attend(1, 0, heads, early, rest_b, slab_rows, place, False)
    returned_b = exchange(blocks_b[0])
    rest_c = after(rest_b, (arrived_a, blocks_b))
    blocks_c = attend(2, 1, heads, early, rest_c, slab_rows, place, True)
    arrived_c = to_chips(blocks_c)

    arrived_a = after(arrived_a, blocks_c)
    swapped = to_cores(arrived_a)
    result = unpack(0, heads, groups, place, arrived_a, 0, ())
    result = unpack(0, heads, groups, place, (swapped,), 1, result)
    result = unpack(1, heads, groups, place, (returned_b,), None, result)
    arrived_c = after(arrived_c, result)
    swapped = to_cores(arrived_c)
    result = unpack(2, heads, groups, place, arrived_c, 0, result)
    result = unpack(2, heads, groups, place, (swapped,), 1, result)
    attended, grads = result
    return attended[None], grads.transpose(1, 0, 2)[None]


def solution(mesh):
    placed = (
        P("dp", "seq", None, None, None),
        P("dp", "seq"),
        P("dp", "seq"),
        P("dp", "seq", None),
    )
    return jax.shard_map(
        local,
        mesh=mesh,
        in_specs=placed,
        out_specs=(P("dp", "seq", None), P("dp", "seq", None, None)),
        check_vma=False,
    )
```

```python
import functools

import jax
import jax.numpy as jnp
from jax import lax
from jax.experimental import pallas as pl
from jax.experimental.pallas import tpu as pltpu
from jax.sharding import PartitionSpec as P

HD = 128
FACTOR = HD ** (-0.5)
LOG2E = 1.4426950408889634
TILE = 16
VMEM_LIMIT = 64 * 1024 * 1024 - 256 * 1024
NT = (((1,), (1,)), ((), ()))
TN = (((0,), (0,)), ((), ()))
NN = (((1,), (0,)), ((), ()))
HBM = pl.BlockSpec(memory_space=pltpu.HBM)
ANY = pl.BlockSpec(memory_space=pl.ANY)
WHOLE = pl.BlockSpec(memory_space=pltpu.VMEM)
SCALARS = pl.BlockSpec(memory_space=pltpu.SMEM)


def dot(left, right, dims=NN):
    return lax.dot_general(left, right, dims, preferred_element_type=jnp.float32)


def one_hot(wanted, shape, dtype):
    slot = lax.broadcasted_iota(jnp.int32, shape, 1)
    return jnp.where(slot == wanted, 1.0, 0.0).astype(dtype)


def floor_to(value, step):
    return pl.multiple_of(lax.div(value, step) * step, step)


def shifted(array, axis, by):
    devices = lax.axis_size(axis)
    pairs = [(i, i + by) for i in range(devices) if 0 <= i + by < devices]
    return lax.ppermute(array, axis, pairs)


def early_start(count, rows):
    return jnp.clip(count - rows * 3 // 4, 0, rows // 4)


def first_kernel(chunks, heads, count_ref, buffer_ref, grad_ref, label_ref, out_ref, *refs):
    ends, refs = refs[: 2 * len(chunks)], refs[2 * len(chunks) :]
    message, window, grad, tail, head, labels, sems = refs[:7]
    priors = refs[7:]
    rows = grad.shape[0]
    half = rows // 2
    margin = head.shape[1]
    capacity = buffer_ref.shape[1]
    groups = out_ref.shape[0]
    count = count_ref[0]
    start = early_start(count, rows)
    base = floor_to(start, TILE)
    reach = window.shape[1]
    tail_start = count - margin
    tail_reach = tail.shape[1]
    tail_base = floor_to(jnp.minimum(tail_start, capacity - tail_reach), TILE)
    copies = [
        pltpu.make_async_copy(grad_ref, grad, sems.at[0]),
        pltpu.make_async_copy(buffer_ref.at[:, pl.ds(base, reach)], window, sems.at[1]),
        pltpu.make_async_copy(buffer_ref.at[:, pl.ds(tail_base, tail_reach)], tail, sems.at[2]),
        pltpu.make_async_copy(buffer_ref.at[:, pl.ds(0, margin)], head, sems.at[3]),
    ]
    for copy in copies:
        copy.start()
    labels[...] = jnp.full(labels.shape, 3.0, jnp.float32)
    for at in range(0, rows, HD):
        wide = min(HD, rows - at)
        labels[at // HD : at // HD + 1, :wide] = label_ref[:, at : at + wide].astype(jnp.float32)
    label_tile = labels[...].astype(out_ref.dtype)
    position = lax.broadcasted_iota(jnp.int32, (half, reach), 0)
    pick = one_hot(position + (start - base), (half, reach), window.dtype)
    sent = []
    copies[0].wait()
    copies[1].wait()
    for group in range(groups):
        columns = slice(group * heads * HD, (group + 1) * heads * HD)
        for h in range(heads):
            column = (group * heads + h) * HD
            message[group, h * rows : (h + 1) * rows] = grad[:, column : column + HD]
        for part in range(3):
            picked = dot(pick, window[part, :, columns]).astype(out_ref.dtype)
            for h in range(heads):
                at = heads * rows + (h * 3 + part) * half
                message[group, at : at + half] = picked[:, h * HD : (h + 1) * HD]
        message[group, heads * (rows + 3 * half) :] = label_tile
        sent.append(pltpu.make_async_copy(message.at[group], out_ref.at[group], sems.at[4 + group]))
        sent[-1].start()
    copies[2].wait()
    copies[3].wait()
    free = 4 + groups
    position = lax.broadcasted_iota(jnp.int32, (margin, tail_reach), 0)
    pick = one_hot(position + (tail_start - tail_base), (margin, tail_reach), tail.dtype)
    for which, (at, number) in enumerate(chunks):
        wide = number * HD
        for group in range(groups):
            source = (group * heads + at) * HD
            target = group * wide
            sent.append(
                pltpu.make_async_copy(
                    head.at[:, :, pl.ds(source, wide)],
                    ends[2 * which + 1].at[:, :, pl.ds(target, wide)],
                    sems.at[free],
                )
            )
            sent[-1].start()
            free += 1
            for part in range(3):
                last = dot(pick, tail[part, :, source : source + wide])
                priors[which][part, :, target : target + wide] = last.astype(tail.dtype)
        sent.append(pltpu.make_async_copy(priors[which], ends[2 * which], sems.at[free]))
        sent[-1].start()
        free += 1
    for copy in sent:
        copy.wait()


def first_parts(live_count, buffer, grad, labels, chunks, groups, heads, margin):
    rows, width = grad.shape
    half = rows // 2
    shapes = [(groups, heads * rows + heads * 3 * half + TILE, HD)]
    priors = []
    for _, number in chunks:
        shape = (3, margin, width // heads * number)
        shapes += [shape, shape]
        priors.append(pltpu.VMEM(shape, buffer.dtype))
    outs = pl.pallas_call(
        functools.partial(first_kernel, chunks, heads),
        out_shape=[jax.ShapeDtypeStruct(shape, buffer.dtype) for shape in shapes],
        in_specs=[SCALARS, HBM, HBM, WHOLE],
        out_specs=[HBM] * len(shapes),
        scratch_shapes=[
            pltpu.VMEM(shapes[0], buffer.dtype),
            pltpu.VMEM((3, half + TILE, width), buffer.dtype),
            pltpu.VMEM((rows, width), grad.dtype),
            pltpu.VMEM((3, margin + TILE, width), buffer.dtype),
            pltpu.VMEM((3, margin, width), buffer.dtype),
            pltpu.VMEM((TILE, HD), jnp.float32),
            pltpu.SemaphoreType.DMA((4 + groups + len(chunks) * (groups + 1),)),
        ]
        + priors,
        compiler_params=pltpu.CompilerParams(vmem_limit_bytes=VMEM_LIMIT),
    )(live_count, buffer, grad, labels)
    return outs[0], [(outs[1 + 2 * i], outs[2 + 2 * i]) for i in range(len(chunks))]


def rest_kernel(chunk, heads, counts_ref, shard_ref, prior_ref, buffer_ref, later_ref, out_ref, message, joined, sems):
    at, number = chunk
    groups = out_ref.shape[0]
    margin = prior_ref.shape[1]
    rows = 4 * margin
    half = 2 * margin
    wide = number * HD
    shard = shard_ref[0]
    count = counts_ref[shard]
    before = lax.fori_loop(0, shard, lambda i, total: total + counts_ref[i], jnp.int32(0))
    lead = before - shard * rows
    own_end = count + lead
    start = early_start(count, rows)
    place = start + lead
    base = floor_to(start + half, TILE)
    reach = half + TILE
    copies = [
        pltpu.make_async_copy(prior_ref, joined.at[:, pl.ds(0, margin)], sems.at[0]),
        pltpu.make_async_copy(later_ref, joined.at[:, pl.ds(half + reach, margin)], sems.at[1]),
    ]
    for group in range(groups):
        columns = pl.ds((group * heads + at) * HD, wide)
        target = pl.ds(group * wide, wide)
        copies.append(
            pltpu.make_async_copy(
                buffer_ref.at[:, pl.ds(0, margin), columns],
                joined.at[:, pl.ds(margin, margin), target],
                sems.at[len(copies)],
            )
        )
        copies.append(
            pltpu.make_async_copy(
                buffer_ref.at[:, pl.ds(base, reach), columns],
                joined.at[:, pl.ds(half, reach), target],
                sems.at[len(copies)],
            )
        )
    for copy in copies:
        copy.start()
    shape = (half, joined.shape[1])
    slot = lax.broadcasted_iota(jnp.int32, shape, 0)
    position = jnp.where(slot < place, slot, slot + half)
    own_row = position - lead
    wanted = jnp.where(
        position >= own_end,
        position - own_end + half + reach,
        jnp.where(slot < place, own_row + margin, own_row - base + half),
    )
    pick = one_hot(wanted, shape, joined.dtype)
    place_tile = jnp.full((TILE, HD), place, jnp.int32).astype(jnp.float32).astype(out_ref.dtype)
    sent = []
    for copy in copies:
        copy.wait()
    for group in range(groups):
        for part in range(3):
            source = joined[part, :, group * wide : (group + 1) * wide]
            picked = dot(pick, source).astype(out_ref.dtype)
            for head in range(number):
                to = (head * 3 + part) * half
                message[group, to : to + half] = picked[:, head * HD : (head + 1) * HD]
        message[group, number * 3 * half :] = place_tile
        sent.append(
            pltpu.make_async_copy(
                message.at[group], out_ref.at[group], sems.at[2 * groups + 2 + group]
            )
        )
        sent[-1].start()
    for copy in sent:
        copy.wait()


def rest_parts(chunk, heads, counts, shard, prior, buffer, later, groups):
    margin = prior.shape[1]
    wide = prior.shape[2]
    total = chunk[1] * 6 * margin + TILE
    return pl.pallas_call(
        functools.partial(rest_kernel, chunk, heads),
        out_shape=jax.ShapeDtypeStruct((groups, total, HD), buffer.dtype),
        in_specs=[SCALARS, SCALARS, ANY, HBM, ANY],
        out_specs=HBM,
        scratch_shapes=[
            pltpu.VMEM((groups, total, HD), buffer.dtype),
            pltpu.VMEM((3, 5 * margin + TILE, wide), buffer.dtype),
            pltpu.SemaphoreType.DMA((3 * groups + 2,)),
        ],
        compiler_params=pltpu.CompilerParams(vmem_limit_bytes=VMEM_LIMIT),
    )(counts, shard, prior, buffer, later)


def clip_of(position, first_end, second_end):
    return jnp.where(position >= first_end, 1, 0) + jnp.where(position >= second_end, 1, 0)


def attend_kernel(
    early_ref,
    rest_ref,
    place_ref,
    upstream_ref,
    label_ref,
    place_in_seq_ref,
    *refs,
):
    outs, refs = refs[:-7], refs[-7:]
    query_rows, key_rows, value_rows, grad_keys, grad_values, results, sems = refs
    groups, rows, _ = upstream_ref.shape
    half = rows // 2
    total = groups * rows
    pair = 2
    block = pair * rows
    labels = label_ref[...].astype(jnp.float32)
    first_end = jnp.sum(jnp.where(labels < 0.5, 1.0, 0.0)).astype(jnp.int32)
    second_end = jnp.sum(jnp.where(labels < 1.5, 1.0, 0.0)).astype(jnp.int32)
    grad_keys[...] = jnp.zeros_like(grad_keys)
    grad_values[...] = jnp.zeros_like(grad_values)

    for group in range(groups):
        place = jnp.max(place_ref[group].astype(jnp.float32)).astype(jnp.int32)
        position = lax.broadcasted_iota(jnp.int32, (rows, rows), 0)
        wanted = jnp.where(
            position < place,
            position + half,
            jnp.where(position < place + half, position - place, position),
        )
        pick = one_hot(wanted, (rows, rows), early_ref.dtype)
        parts = [
            jnp.concatenate(
                [
                    early_ref[group, part * half : (part + 1) * half],
                    rest_ref[group, part * half : (part + 1) * half],
                ],
                axis=0,
            )
            for part in range(3)
        ]
        whole = dot(pick, jnp.concatenate(parts, axis=1)).astype(early_ref.dtype)
        span = pl.ds(group * rows, rows)
        query_rows[span] = whole[:, :HD]
        key_rows[span] = whole[:, HD : 2 * HD]
        value_rows[span] = whole[:, 2 * HD :]

    def on_keys(i, low, reach):
        begin = pl.multiple_of(jnp.minimum(low, total - reach), HD) if reach < total else 0
        keys = pl.ds(begin, reach)
        queries = query_rows[pl.ds(pl.multiple_of(i * block, block), block)]
        upstream = upstream_ref[pl.ds(i * pair, pair)].reshape(block, HD)
        scores = dot(queries, key_rows[keys], NT)
        grad_probs = dot(upstream, value_rows[keys], NT)
        row_at = i * block + lax.broadcasted_iota(jnp.int32, (block, 1), 0)
        key_at = begin + lax.broadcasted_iota(jnp.int32, (1, reach), 1)
        same_clip = clip_of(row_at, first_end, second_end) == clip_of(key_at, first_end, second_end)
        scores = jnp.where(same_clip, scores, -1e30)
        row_top = jnp.max(scores, axis=1, keepdims=True)
        weights = jnp.exp2((scores - row_top) * (FACTOR * LOG2E))
        probs = weights * (1.0 / jnp.sum(weights, axis=1, keepdims=True))
        probs_low = probs.astype(jnp.bfloat16)
        row_inner = jnp.sum(probs * grad_probs, axis=1, keepdims=True)
        grad_scores = (probs * (grad_probs - row_inner) * FACTOR).astype(jnp.bfloat16)
        mixed = dot(probs_low, value_rows[keys]).astype(results.dtype)
        grad_queries = dot(grad_scores, key_rows[keys]).astype(results.dtype)
        results[pl.ds(i * pair, pair), 0] = mixed.reshape(pair, rows, HD)
        results[pl.ds(i * pair, pair), 1] = grad_queries.reshape(pair, rows, HD)
        grad_keys[:, keys] += dot(queries, grad_scores, TN)
        grad_values[:, keys] += dot(upstream, probs_low, TN)

    def one(i, carry):
        begin = i * block
        last = begin + block - 1
        low = jnp.where(
            begin >= second_end, second_end, jnp.where(begin >= first_end, first_end, 0)
        )
        high = jnp.where(
            last < first_end, first_end, jnp.where(last < second_end, second_end, total)
        )
        low = lax.div(low, HD) * HD
        span = high - low
        covered = 0
        for reach in (total // 4, total // 4 + 2 * HD, total // 2 + HD, total - 2 * HD, total):
            pl.when((span > covered) & (span <= reach))(functools.partial(on_keys, i, low, reach))
            covered = reach
        return carry

    lax.fori_loop(0, groups // pair, one, 0)
    results[:, 2] = grad_keys[...].T.reshape(groups, rows, HD).astype(results.dtype)
    results[:, 3] = grad_values[...].T.reshape(groups, rows, HD).astype(results.dtype)
    copies = []
    if len(outs) == 1:
        copies.append(pltpu.make_async_copy(results, outs[0], sems.at[0]))
    for ahead, out in enumerate(outs if len(outs) > 1 else ()):
        for other in range(2):
            source = results.at[group_at(place_in_seq_ref[0], groups, ahead, other)]
            sem = sems.at[len(copies)]
            copies.append(pltpu.make_async_copy(source, out.at[other], sem))
    for copy in copies:
        copy.start()
    for copy in copies:
        copy.wait()


def group_at(place, groups, ahead, other):
    core = lax.rem(place, 2)
    chip = lax.rem(lax.div(place, 2) + ahead, groups // 2)
    return 2 * chip + (1 - core if other else core)


def attend(head, local_head, heads, early, rest, rows, place, parted):
    groups = early.shape[0]
    total = groups * rows
    half = rows // 2
    early_at = heads * rows // (3 * half)
    label_at = heads * (rows + 3 * half) // TILE
    place_at = rest.shape[1] // TILE - 1
    if parted:
        shapes = [(2, 4, rows, HD)] * (groups // 2)
    else:
        shapes = [(groups, 4, rows, HD)]
    return pl.pallas_call(
        attend_kernel,
        out_shape=[jax.ShapeDtypeStruct(shape, early.dtype) for shape in shapes],
        grid=(1,),
        in_specs=[
            pl.BlockSpec((groups, 3 * half, HD), lambda h: (0, early_at + head, 0)),
            pl.BlockSpec((groups, 3 * half, HD), lambda h: (0, local_head, 0)),
            pl.BlockSpec((groups, TILE, HD), lambda h: (0, place_at, 0)),
            pl.BlockSpec((groups, rows, HD), lambda h: (0, head, 0)),
            pl.BlockSpec((groups, TILE, HD), lambda h: (0, label_at, 0)),
            SCALARS,
        ],
        out_specs=[HBM] * len(shapes),
        scratch_shapes=[pltpu.VMEM((total, HD), early.dtype)] * 3
        + [pltpu.VMEM((HD, total), jnp.float32)] * 2
        + [pltpu.VMEM((groups, 4, rows, HD), early.dtype), pltpu.SemaphoreType.DMA((groups,))],
        compiler_params=pltpu.CompilerParams(vmem_limit_bytes=VMEM_LIMIT),
        cost_estimate=pl.CostEstimate(
            flops=10 * total * total * HD,
            bytes_accessed=16 * total * HD,
            transcendentals=total * total,
        ),
    )(early, rest, rest, early, early, place)


def others_kernel(*refs):
    parts, out_ref, held, sems = refs[:-3], refs[-3], refs[-2], refs[-1]
    number = len(parts)
    loads = []
    for i, part in enumerate(parts):
        loads.append(pltpu.make_async_copy(part.at[1], held.at[i], sems.at[i]))
        loads[-1].start()
    stores = []
    for i in range(number):
        loads[i].wait()
        stores.append(pltpu.make_async_copy(held.at[i], out_ref.at[i], sems.at[number + i]))
        stores[-1].start()
    for store in stores:
        store.wait()


def others_of(parts):
    shape = (len(parts), *parts[0].shape[1:])
    return pl.pallas_call(
        others_kernel,
        out_shape=jax.ShapeDtypeStruct(shape, parts[0].dtype),
        in_specs=[ANY] * len(parts),
        out_specs=HBM,
        scratch_shapes=[
            pltpu.VMEM(shape, parts[0].dtype),
            pltpu.SemaphoreType.DMA((2 * len(parts),)),
        ],
        compiler_params=pltpu.CompilerParams(vmem_limit_bytes=VMEM_LIMIT),
    )(*parts)


def unpack_kernel(head, heads, groups, other, number, place_ref, *refs):
    sources = refs[:number]
    attended_ref, grads_ref, held, sems = refs[-4:]
    blocks = []
    if other is None:
        blocks = [(sources[0].at[group], group) for group in range(groups)]
    for back in range(0 if other is None else groups // 2):
        ahead = (groups // 2 - back) % (groups // 2)
        block = sources[0].at[back] if other else sources[back].at[0]
        blocks.append((block, group_at(place_ref[0], groups, ahead, other)))
    loads = []
    for i, (block, _) in enumerate(blocks):
        loads.append(pltpu.make_async_copy(block, held.at[i], sems.at[i]))
        loads[-1].start()
    stores = []
    for i, (_, group) in enumerate(blocks):
        loads[i].wait()
        columns = pl.ds(pl.multiple_of((group * heads + head) * HD, HD), HD)
        first = sems.at[len(blocks) + 2 * i]
        second = sems.at[len(blocks) + 2 * i + 1]
        stores.append(pltpu.make_async_copy(held.at[i, 0], attended_ref.at[:, columns], first))
        stores.append(
            pltpu.make_async_copy(held.at[i, pl.ds(1, 3)], grads_ref.at[:, :, columns], second)
        )
        stores[-2].start()
        stores[-1].start()
    for store in stores:
        store.wait()


def unpack(head, heads, groups, place, sources, other, so_far):
    _, _, rows, _ = sources[0].shape
    width = groups * heads * HD
    dtype = sources[0].dtype
    number = len(sources)
    return pl.pallas_call(
        functools.partial(unpack_kernel, head, heads, groups, other, number),
        out_shape=[
            jax.ShapeDtypeStruct((rows, width), dtype),
            jax.ShapeDtypeStruct((3, rows, width), dtype),
        ],
        in_specs=[SCALARS] + [ANY] * number + [HBM] * len(so_far),
        out_specs=[HBM, HBM],
        scratch_shapes=[
            pltpu.VMEM((groups, 4, rows, HD), dtype),
            pltpu.SemaphoreType.DMA((3 * groups,)),
        ],
        input_output_aliases={1 + number: 0, 2 + number: 1} if so_far else {},
        compiler_params=pltpu.CompilerParams(vmem_limit_bytes=VMEM_LIMIT),
    )(place, *sources, *so_far)


def to_chips(parts):
    places = lax.axis_size("seq")
    arrived = [parts[0]]
    for ahead in range(1, len(parts)):
        pairs = [(i, (i + 2 * ahead) % places) for i in range(places)]
        arrived.append(lax.ppermute(parts[ahead], "seq", pairs))
    return arrived


def to_cores(arrived):
    swap = [(i, i ^ 1) for i in range(lax.axis_size("seq"))]
    return lax.ppermute(others_of(arrived), "seq", swap)


def after(array, first):
    return lax.optimization_barrier((array, first))[0]


def exchange(array):
    return lax.all_to_all(array, "seq", split_axis=0, concat_axis=0, tiled=True)


def local(source_rows, shard_counts, segment_ids, out_grad):
    buffer = source_rows[0, 0].transpose(1, 0, 2)
    live_count = shard_counts[0]
    slab_rows = out_grad.shape[1]
    margin = slab_rows // 4
    groups = lax.axis_size("seq")
    heads = out_grad.shape[2] // HD // groups
    chunks = [(0, 1), (1, heads - 1)]
    shard = lax.axis_index("dp").astype(jnp.int32)[None]
    place = lax.axis_index("seq").astype(jnp.int32)[None]

    message, ends = first_parts(
        live_count, buffer, out_grad[0], segment_ids, chunks, groups, heads, margin
    )
    early = exchange(message)
    first_ends, own_count = lax.optimization_barrier((ends[0], live_count))
    halos = [(shifted(first_ends[0], "dp", 1), shifted(first_ends[1], "dp", -1))]
    indices = jnp.arange(lax.axis_size("dp"), dtype=jnp.int32)
    counts = lax.psum(jnp.where(indices == shard, own_count, 0), "dp")
    later_ends, counts = lax.optimization_barrier((ends[1:], counts))
    for prior, later in later_ends:
        halos.append((shifted(prior, "dp", 1), shifted(later, "dp", -1)))

    received = []
    for chunk, (prior, later) in zip(chunks, halos):
        rest = rest_parts(chunk, heads, counts, shard, prior, buffer, later, groups)
        rest, early = lax.optimization_barrier((rest, early))
        received.append(exchange(rest))
    rest_a, rest_b = received
    blocks_a = attend(0, 0, heads, early, rest_a, slab_rows, place, True)
    arrived_a = to_chips(blocks_a)
    rest_b = after(rest_b, blocks_a)
    blocks_b = attend(1, 0, heads, early, rest_b, slab_rows, place, False)
    returned_b = exchange(blocks_b[0])
    rest_c = after(rest_b, (arrived_a, blocks_b))
    blocks_c = attend(2, 1, heads, early, rest_c, slab_rows, place, True)
    arrived_c = to_chips(blocks_c)

    arrived_a = after(arrived_a, blocks_c)
    swapped = to_cores(arrived_a)
    result = unpack(0, heads, groups, place, arrived_a, 0, ())
    result = unpack(0, heads, groups, place, (swapped,), 1, result)
    result = unpack(1, heads, groups, place, (returned_b,), None, result)
    arrived_c = after(arrived_c, result)
    swapped = to_cores(arrived_c)
    result = unpack(2, heads, groups, place, arrived_c, 0, result)
    result = unpack(2, heads, groups, place, (swapped,), 1, result)
    attended, grads = result
    return attended[None], grads.transpose(1, 0, 2)[None]


def solution(mesh):
    placed = (
        P("dp", "seq", None, None, None),
        P("dp", "seq"),
        P("dp", "seq"),
        P("dp", "seq", None),
    )
    return jax.shard_map(
        local,
        mesh=mesh,
        in_specs=placed,
        out_specs=(P("dp", "seq", None), P("dp", "seq", None, None)),
        check_vma=False,
    )
```
